512 devices in a mesh: grp: 32 (over x, z), tp: 16 (over y, core).
Axes of the slice: x: 4, y: 8, z: 8, core: 2. Of those that a mesh axis runs over, the one named last changes fastest.
Arguments:
- acts: bfloat16 [4096, 8192], P('grp', 'tp'), may hold values from -6 to 6
- grads: bfloat16 [4096, 4096], P('grp'), may hold values from -1.5 to 1.5
- counts: int32 [32, 24], P('grp'), may hold values from 1 to 12, 128 in all within a row
- owner_slot: int32 [24], replicated, may hold values from 0 to 31, as said below
- base_weight: bfloat16 [8192, 4096], P('tp', 'grp')
- adapter_a: bfloat16 [32, 8192, 32], P('grp', 'tp'), may hold values from -0.0625 to 0.0625
- adapter_b: bfloat16 [32, 32, 4096], P('grp'), may hold values from -0.59765625 to 0.59765625
- magnitude: float32 [32, 4096], P('grp'), may hold values from 0.5 to 2
Outputs:
- row_grad: bfloat16 [4096, 8192], P('grp', 'tp')
- grad_a: float32 [32, 8192, 32], P('grp', 'tp')
- grad_b: float32 [32, 32, 4096], P('grp', None, 'tp')
- grad_gain: float32 [32, 4096], P('grp')
The draws below stay inside these ranges and needn't reach their ends.
Inputs may be any that keep to these rules, and one draw needn't show every extreme that they name: Every tenant has one row or more on every index of grp; the largest count in each row of counts is exactly 12. `owner_slot`: distinct slots, one for each tenant; slot p lies on index p // 1 of grp; other slots are unused.
All inputs are finite; a program needn't handle non-finite values.
Results may differ from the reference program's by a relative error of at most 0.0095.
Values may be sent and summed in bfloat16 or wider, within the bound.
No kernel may reach another device: no remote copies, remote signals or barrier semaphores. Data moves between devices by JAX's collectives and lax.ppermute only.
A program may use at most 64 MiB of HBM per device.

```python
import math
import jax
import jax.numpy as jnp
import numpy as np
from jax import lax

D = 8192
DOUT = 4096
R = 32
TENANTS = 24
TOK_DEV = 128
CAP = 12
SLOT_ALL = 32
TOKENS = 4096
N_GRP = 32


def draw_owner_slot(key, part):
    key = jax.random.fold_in(key, 7)
    return jax.random.permutation(key, SLOT_ALL)[:TENANTS].astype(jnp.int32)


def draw_base_weight(key, part):
    key = jax.random.fold_in(key, 11)
    key_main, key_rough = jax.random.split(key, 2)
    position = jnp.arange(D, dtype=jnp.float32) / D
    rising = jnp.exp(position * math.log(3.0))[:, None]
    rough = jnp.exp(jax.random.uniform(key_rough, (D, 1), jnp.float32, 0.0, math.log(3.5)))
    entries = jax.random.normal(key_main, (D, DOUT), jnp.float32)
    return (entries * rising * rough / math.sqrt(D)).astype(jnp.bfloat16)


def block_scale(stream_key, extent, cuts, least, largest):
    loudness = 1.0
    for dim, blocks in cuts:
        heights = jax.random.uniform(jax.random.fold_in(jax.random.fold_in(stream_key, 6), dim), (blocks,), jnp.float32, least / len(cuts), largest / len(cuts))
        loudness = loudness * jnp.repeat(jnp.exp(heights), extent[dim] // blocks).reshape((-1,) + (1,) * (len(extent) - 1 - dim))
    return loudness


def length_profile(number_of, total, bound, skew):
    weights = [(1 << 20) // math.isqrt(rank ** skew) + 1 for rank in range(2, number_of + 1)]
    rest, holding = total - bound - (number_of - 1), [1] * (number_of - 1)
    while rest > 0:
        free = [i for i in range(number_of - 1) if holding[i] < bound]
        pool, left = sum([weights[i] for i in free]), rest
        for i in free:
            addition = min(bound - holding[i], max(1, left * weights[i] // pool), rest)
            holding[i] = holding[i] + addition
            rest = rest - addition
    return np.array([bound] + holding)


def ragged(key, amount, total, limit, slope):
    if amount == 2:
        one = jax.random.randint(key, (), max(1, total - limit), min(limit, total - 1) + 1)
        return jnp.stack([one, total - one])
    lengths = jnp.asarray(length_profile(amount, total, limit, slope), jnp.int32)
    couples = (amount - 1) // 2
    giver, taker = lengths[1:1 + 2 * couples:2], lengths[2:2 + 2 * couples:2]
    room = jnp.minimum(giver - 1, limit - taker)
    passed = jax.random.randint(jax.random.fold_in(key, 1), (couples,), 0, 1 << 20) % (room + 1)
    lengths = lengths.at[1:1 + 2 * couples:2].set(giver - passed).at[2:2 + 2 * couples:2].set(taker + passed)
    return lengths[jax.random.permutation(jax.random.fold_in(key, 2), amount)]


def gaussian(key, dims, spread, most, cuts=(), held_as=jnp.bfloat16):
    factor_of = block_scale(key, dims, cuts, -0.22, 0.18) if cuts else 1.0
    result = jax.random.normal(key, dims, jnp.float32) * spread * factor_of
    return jnp.minimum(jnp.maximum(result, -most), most).astype(held_as)


def setup_inputs(seed: int = 0) -> dict:
    splits = jax.random.split(jax.random.key(seed), 9)
    acts = gaussian(splits[0], (TOKENS, D), 1.0, 6.0, ((0, 32), (1, 16)))
    grads = gaussian(splits[1], (TOKENS, DOUT), 0.25, 1.5, ((0, 32),))
    counts = jax.vmap(lambda own: ragged(own, TENANTS, TOK_DEV, CAP, 2))(jax.random.split(splits[2], N_GRP)).reshape((N_GRP, TENANTS)).astype(jnp.int32)
    owner_slot = draw_owner_slot(jax.random.fold_in(splits[8], 71), 0)
    base_weight = draw_base_weight(jax.random.fold_in(splits[8], 71), 0)
    adapter_a = gaussian(splits[5], (SLOT_ALL, D, R), D ** -0.5, 0.0625, ((0, 32), (1, 16)))
    adapter_b = gaussian(splits[6], (SLOT_ALL, R, DOUT), 0.1, 0.59765625, ((0, 32),))
    magnitude = jnp.clip(jnp.exp(math.log(2.0) - 1.3862944 * jax.random.uniform(splits[7], (SLOT_ALL, DOUT), jnp.float32) ** block_scale(splits[7], (SLOT_ALL, DOUT), ((0, 32),), -0.2, 0.2)), 0.5, 2.0)
    return dict(acts=acts, grads=grads, counts=counts, owner_slot=owner_slot, base_weight=base_weight, adapter_a=adapter_a, adapter_b=adapter_b, magnitude=magnitude)


PRECISE = lax.Precision.HIGHEST
EPSILON = 1e-06

def reference(acts, grads, counts, owner_slot, base_weight, adapter_a, adapter_b, magnitude):
    row_ends = jnp.cumsum(counts, axis=1).astype(jnp.int32)
    row_starts = row_ends - counts
    weight = base_weight.astype(jnp.float32)
    offsets = jnp.arange(CAP, dtype=jnp.int32)
    device_base = (jnp.arange(N_GRP, dtype=jnp.int32) * TOK_DEV)[:, None]

    def per_tenant(tenant):
        slot_index = owner_slot[tenant]
        first_fac = adapter_a[slot_index]
        second_fac = adapter_b[slot_index]
        gain = magnitude[slot_index]
        merged = weight + jnp.dot(first_fac, second_fac, preferred_element_type=jnp.float32)
        column_norm = jnp.sqrt(lax.optimization_barrier(jnp.sum(merged * merged, axis=0)) + EPSILON)
        first_row = row_starts[:, tenant][:, None]
        number = counts[:, tenant][:, None]
        valid = (offsets[None, :] < number).reshape(-1)
        gather_at = jnp.where(valid, (device_base + first_row + offsets[None, :]).reshape(-1), 0).astype(jnp.int32)
        rows_in = jnp.where(valid[:, None], acts[gather_at], jnp.zeros((), jnp.bfloat16))
        rows_grad = jnp.where(valid[:, None], grads[gather_at], jnp.zeros((), jnp.bfloat16))
        moment = lax.dot_general(rows_in, rows_grad, (((0,), (0,)), ((), ())), preferred_element_type=jnp.float32)
        align = lax.optimization_barrier(jnp.sum(merged * moment, axis=0))
        scale = gain / column_norm
        d_gain = align / column_norm
        shrink = gain * align / (column_norm * column_norm * column_norm)
        d_merged = moment * scale[None, :] - merged * shrink[None, :]
        d_first = jnp.dot(d_merged, second_fac.astype(jnp.float32).T, precision=PRECISE)
        d_second = jnp.dot(first_fac.astype(jnp.float32).T, d_merged, precision=PRECISE)
        return (d_first, d_second, d_gain, scale)
    d_first, d_second, d_gain, scales = lax.map(per_tenant, jnp.arange(TENANTS, dtype=jnp.int32))
    grad_a = jnp.zeros((SLOT_ALL, D, R), jnp.float32).at[owner_slot].set(d_first)
    grad_b = jnp.zeros((SLOT_ALL, R, DOUT), jnp.float32).at[owner_slot].set(d_second)
    grad_gain = jnp.zeros((SLOT_ALL, DOUT), jnp.float32).at[owner_slot].set(d_gain)
    local_rows = jnp.arange(TOK_DEV, dtype=jnp.int32)
    row_tenant = lax.optimization_barrier(jnp.sum((local_rows[None, :, None] >= row_ends[:, None, :]).astype(jnp.int32), axis=2)).reshape(-1)
    one_hot = (row_tenant[:, None] == jnp.arange(TENANTS, dtype=jnp.int32)[None, :]).astype(jnp.float32)
    row_scale = jnp.dot(one_hot, scales, precision=PRECISE)
    hidden = (grads.astype(jnp.float32) * row_scale).astype(jnp.bfloat16)
    main_part = lax.dot_general(hidden, base_weight, (((1,), (1,)), ((), ())), preferred_element_type=jnp.float32)

    def add_low(total, tenant):
        slot_index = owner_slot[tenant]
        inner = lax.dot_general(hidden, adapter_b[slot_index], (((1,), (1,)), ((), ())), preferred_element_type=jnp.float32)
        inner = jnp.where((row_tenant == tenant)[:, None], inner, 0.0).astype(jnp.bfloat16)
        low_part = lax.dot_general(inner, adapter_a[slot_index], (((1,), (1,)), ((), ())), preferred_element_type=jnp.float32)
        return (total + low_part, None)
    low_total, unused = lax.scan(add_low, jnp.zeros((TOKENS, D), jnp.float32), jnp.arange(TENANTS, dtype=jnp.int32))
    row_grad = (main_part + low_total).astype(jnp.bfloat16)
    return (row_grad, grad_a, grad_b, grad_gain)
```

```python
import jax
import jax.numpy as jnp
from jax import lax
from jax.sharding import PartitionSpec as P

CAP = 12
NX = 4
EPSILON = 1e-06
HIGH = lax.Precision.HIGHEST
BF = jnp.bfloat16
F32 = jnp.float32


def dot(left, right, dims, precision=None):
    return lax.dot_general(
        left, right, (dims, ((), ())), precision=precision, preferred_element_type=F32
    )


def split_pair(values):
    upper = values.astype(BF)
    return upper, (values - upper.astype(F32)).astype(BF)


def row_targets(count_row, owner_slot, rows):
    ends = jnp.cumsum(count_row)
    starts = ends - count_row
    ids = jnp.arange(rows, dtype=jnp.int32)[None, :]
    inside = ((ids >= starts[:, None]) & (ids < ends[:, None])).astype(jnp.int32)
    shift = owner_slot * CAP - starts
    return jnp.sum(inside * shift[:, None], axis=0) + ids[0]


def on_device(acts, grads, counts, owner_slot, base_weight, adapter_a, adapter_b, magnitude):
    groups, shards = lax.axis_size("grp"), lax.axis_size("tp")
    nz = groups // NX
    quads = shards // NX
    rows, width = acts.shape
    out_width = grads.shape[1]
    rank = adapter_a.shape[2]
    x_cols, t_cols = out_width // NX, out_width // shards
    packed = groups * CAP
    z_groups = [[i * nz + j for j in range(nz)] for i in range(NX)]
    x_groups = [[i * nz + j for i in range(NX)] for j in range(nz)]
    my_x = lax.axis_index("grp") // nz
    my_t = lax.axis_index("tp")

    weight_x = lax.all_gather(
        base_weight.T, "grp", axis=0, tiled=True, axis_index_groups=z_groups
    )

    target = row_targets(counts[0], owner_slot, rows)
    place = (jnp.arange(packed, dtype=jnp.int32)[:, None] == target[None, :]).astype(BF)
    grads_t = lax.dynamic_slice(grads, (0, my_t * t_cols), (rows, t_cols))
    both = dot(place, jnp.concatenate([acts, grads_t], axis=1), ((1,), (0,))).astype(BF)
    both = lax.all_to_all(
        both.reshape(groups, CAP, width + t_cols), "grp", split_axis=0, concat_axis=0, tiled=True
    ).reshape(packed, width + t_cols)
    rows_in, rows_grad_t = both[:, :width], both[:, width:]
    rows_grad = lax.all_gather(rows_grad_t, "tp", axis=1, tiled=True)

    first, second = adapter_a[0], adapter_b[0]
    first_t = first.T
    fields = jnp.concatenate(
        [
            jnp.broadcast_to(first_t[None], (NX, rank, width)),
            second.reshape(rank, NX, x_cols).transpose(1, 0, 2),
        ],
        axis=2,
    )
    fields = lax.all_to_all(
        fields, "grp", split_axis=0, concat_axis=0, tiled=True, axis_index_groups=x_groups
    ).reshape(NX * rank, width + x_cols)
    first_all, second_all = fields[:, :width], fields[:, width:]
    second_wide = second_all.astype(F32)

    owner = jnp.arange(NX * rank, dtype=jnp.int32) // rank
    gram = jnp.where(
        owner[:, None] == owner[None, :], dot(first_all, first_all, ((1,), (1,))), 0.0
    )
    gram_second = dot(gram, second_wide, ((1,), (0,)), HIGH)
    first_weight = dot(first_all, weight_x, ((1,), (1,)))
    square_base = jnp.sum(jnp.square(weight_x.astype(F32)), axis=1)
    squares = square_base[None, :] + jnp.sum(
        (second_wide * (2.0 * first_weight + gram_second)).reshape(NX, rank, x_cols), axis=1
    )
    first_merged = first_weight + gram_second
    rows_low = dot(first_t, rows_in, ((1,), (1,)))

    def lanes(values):
        return jnp.concatenate(
            [values[:, i : i + 128] for i in range(0, values.shape[1], 128)], axis=0
        )

    pieces = first_merged.astype(BF).reshape(NX, rank, quads, t_cols)
    pieces = pieces.transpose(0, 2, 1, 3).reshape(shards, rank, t_cols)
    pieces = jnp.concatenate([pieces[:, :, i : i + 128] for i in range(0, t_cols, 128)], axis=1)
    square_upper, square_lower = split_pair(squares)
    common = jnp.concatenate(
        [lanes(square_upper), lanes(square_lower), lanes(rows_low.astype(BF))], axis=0
    )
    sums = jnp.concatenate(
        [pieces, jnp.broadcast_to(common[None], (shards,) + common.shape)], axis=1
    )
    sums = lax.all_to_all(sums, "tp", split_axis=0, concat_axis=0, tiled=True)
    sums = jnp.sum(sums.astype(F32), axis=0)

    def unlanes(values, height):
        return jnp.concatenate(
            [values[i : i + height] for i in range(0, values.shape[0], height)], axis=1
        )

    n_piece = rank * t_cols // 128
    n_square = NX * x_cols // 128
    merged_piece = unlanes(sums[:n_piece], rank)
    square_sum = unlanes(
        sums[n_piece : n_piece + n_square] + sums[n_piece + n_square : n_piece + 2 * n_square], NX
    )
    rows_low = unlanes(sums[n_piece + 2 * n_square :], rank)

    square_own = lax.all_to_all(
        square_sum.reshape(NX, 1, x_cols),
        "grp",
        split_axis=0,
        concat_axis=0,
        tiled=True,
        axis_index_groups=x_groups,
    ).reshape(1, out_width)
    swap = []
    for i in range(NX):
        for j in range(nz):
            for a in range(NX):
                for q in range(quads):
                    swap.append(
                        ((i * nz + j) * shards + a * quads + q, (a * nz + j) * shards + i * quads + q)
                    )
    merged_own = lax.ppermute(merged_piece, ("grp", "tp"), swap)
    norm = jnp.sqrt(square_own + EPSILON)
    scale = magnitude / norm

    def along_x(values, step):
        pairs = [
            (((i + step) % NX) * nz + j, i * nz + j) for i in range(NX) for j in range(nz)
        ]
        return lax.ppermute(values, "grp", pairs)

    after = along_x(weight_x, 1)
    before = along_x(weight_x, -1)
    half = x_cols // 2
    across = jnp.concatenate([along_x(after[:half], 1), along_x(before[half:], -1)], axis=0)
    weight = jnp.zeros((out_width, width), BF)
    for piece, step in ((weight_x, 0), (after, 1), (across, 2), (before, 3)):
        weight = lax.dynamic_update_slice(weight, piece, (((my_x + step) % NX) * x_cols, 0))

    hidden = (rows_grad.astype(F32) * scale).astype(BF)
    inner = dot(hidden, second, ((1,), (1,))).astype(BF)
    back = dot(hidden, weight, ((1,), (0,))) + dot(inner, first, ((1,), (1,)))
    back = lax.all_to_all(
        back.astype(BF).reshape(groups, CAP, width), "grp", split_axis=0, concat_axis=0, tiled=True
    ).reshape(packed, width)
    row_grad = dot(place, back, ((0,), (0,))).astype(BF)

    projected = dot(rows_in, weight, ((1,), (1,)))
    align = jnp.sum(rows_grad.astype(F32) * projected, axis=0)
    second_t = lax.dynamic_slice(second, (0, my_t * t_cols), (rank, t_cols)).astype(F32)
    first_moment = dot(rows_low.astype(BF), rows_grad_t, ((1,), (0,)))
    align_low = jnp.sum(first_moment * second_t, axis=0)
    align_t = lax.dynamic_slice(align, (my_t * t_cols,), (t_cols,)) + align_low
    align = lax.dynamic_update_slice(align, align_t, (my_t * t_cols,))
    align_all = lax.all_to_all(
        jnp.broadcast_to(align.reshape(1, -1, 128), (shards, out_width // 128, 128)),
        "tp",
        split_axis=0,
        concat_axis=0,
        tiled=True,
    )
    align = jnp.sum(align_all, axis=0).reshape(1, out_width)
    grad_gain = align / norm
    shrink = magnitude * align / (norm * norm * norm)

    shrunk = (second.astype(F32) * shrink).astype(BF)
    small = dot(second, shrunk, ((1,), (1,)))
    grad_a = (
        dot(rows_in, inner, ((0,), (0,)))
        - dot(weight, shrunk, ((0,), (1,)))
        - dot(first, small.astype(BF), ((1,), (0,)))
    )
    scale_t = lax.dynamic_slice(scale, (0, my_t * t_cols), (1, t_cols))
    shrink_t = lax.dynamic_slice(shrink, (0, my_t * t_cols), (1, t_cols))
    grad_b = first_moment * scale_t - merged_own * shrink_t
    return row_grad, grad_a[None], grad_b[None], grad_gain


def solution(mesh):
    in_specs = (
        P("grp", "tp"),
        P("grp", None),
        P("grp", None),
        P(),
        P("tp", "grp"),
        P("grp", "tp", None),
        P("grp", None, None),
        P("grp", None),
    )
    out_specs = (P("grp", "tp"), P("grp", "tp", None), P("grp", None, "tp"), P("grp", None))
    return jax.shard_map(
        on_device, mesh=mesh, in_specs=in_specs, out_specs=out_specs, check_vma=False
    )
```

```python
import jax
import jax.numpy as jnp
from jax import lax
from jax.experimental import pallas as pl
from jax.experimental.pallas import tpu as pltpu
from jax.sharding import PartitionSpec as P

CAP = 12
NX = 4
EPSILON = 1e-06
HIGH = lax.Precision.HIGHEST
BF = jnp.bfloat16
F32 = jnp.float32


def dot(left, right, dims, precision=None):
    return lax.dot_general(
        left, right, (dims, ((), ())), precision=precision, preferred_element_type=F32
    )


def split_pair(values):
    upper = values.astype(BF)
    return upper, (values - upper.astype(F32)).astype(BF)


def row_targets(count_row, owner_slot, rows):
    ends = jnp.cumsum(count_row)
    starts = ends - count_row
    ids = jnp.arange(rows, dtype=jnp.int32)[None, :]
    inside = ((ids >= starts[:, None]) & (ids < ends[:, None])).astype(jnp.int32)
    shift = owner_slot * CAP - starts
    return jnp.sum(inside * shift[:, None], axis=0) + ids[0]


def main_kernel(place, scale, second, weight, mine, other, total, low, total_out, low_out):
    step = pl.program_id(0)
    t_cols = mine.shape[2]
    near = place[2] * t_cols
    far = t_cols - near

    @pl.when(step == 0)
    def _():
        total_out[...] = total[...]
        low_out[...] = low[...]

    for start, rows_grad in ((near, mine), (far, other)):
        cols = pl.ds(pl.multiple_of(start, t_cols), t_cols)
        hidden = (rows_grad[0].astype(F32) * scale[:, cols]).astype(BF)
        total_out[...] += jnp.dot(hidden, weight[cols, :], preferred_element_type=F32)
        low_out[...] += dot(hidden, second[:, cols], ((1,), (1,)))


def align_kernel(place, rows_in, weight, mine, other, align_out):
    t_cols = mine.shape[2]
    near = place[2] * t_cols
    far = t_cols - near
    for start, rows_grad in ((near, mine), (far, other)):
        cols = pl.ds(pl.multiple_of(start, t_cols), t_cols)
        projected = dot(rows_in[...], weight[cols, :], ((1,), (1,)))
        align_out[:, cols] = jnp.sum(
            rows_grad[0].astype(F32) * projected, axis=0, keepdims=True
        )


def on_device(acts, grads, counts, owner_slot, base_weight, adapter_a, adapter_b, magnitude):
    groups, shards = lax.axis_size("grp"), lax.axis_size("tp")
    nz = groups // NX
    quads = shards // NX
    rows, width = acts.shape
    out_width = grads.shape[1]
    rank = adapter_a.shape[2]
    x_cols, t_cols = out_width // NX, out_width // shards
    packed = groups * CAP
    z_groups = [[i * nz + j for j in range(nz)] for i in range(NX)]
    x_groups = [[i * nz + j for i in range(NX)] for j in range(nz)]
    my_x = lax.axis_index("grp") // nz
    my_t = lax.axis_index("tp")

    def to_owners(values):
        values = values.reshape(groups, CAP, values.shape[1])
        values = lax.all_to_all(values, "grp", split_axis=0, concat_axis=0, tiled=True)
        return values.reshape(packed, values.shape[2])

    weight_x = lax.all_gather(
        base_weight.T, "grp", axis=0, tiled=True, axis_index_groups=z_groups
    )

    target = row_targets(counts[0], owner_slot, rows)
    place = (jnp.arange(packed, dtype=jnp.int32)[:, None] == target[None, :]).astype(BF)
    grads_t = lax.dynamic_slice(grads, (0, my_t * t_cols), (rows, t_cols))
    grads_t = dot(place, grads_t, ((1,), (0,))).astype(BF)
    rows_grad_t = to_owners(grads_t)
    acts_t = dot(place, acts, ((1,), (0,))).astype(BF)

    ny = shards // 2

    def along_y(values, step):
        pairs = [((i + 2 * step) % shards, i) for i in range(shards)]
        return lax.ppermute(values, "tp", pairs)

    upper, lower = [rows_grad_t], [rows_grad_t]
    for _ in range((ny - 1) // 2):
        upper.append(along_y(upper[-1], 1))
        lower.append(along_y(lower[-1], -1))
    half = packed // 2
    last = jnp.concatenate([along_y(upper[-1][:half], 1), along_y(lower[-1][half:], -1)], axis=0)
    mine = jnp.stack(upper + [last] + lower[:0:-1])
    other = lax.ppermute(mine, "tp", [(i, i ^ 1) for i in range(shards)])

    first, second = adapter_a[0], adapter_b[0]
    first_t = first.T
    fields = jnp.concatenate(
        [
            jnp.broadcast_to(first_t[None], (NX, rank, width)),
            second.reshape(rank, NX, x_cols).transpose(1, 0, 2),
        ],
        axis=2,
    )
    fields, rows_grad_t = lax.optimization_barrier((fields, rows_grad_t))
    fields = lax.all_to_all(
        fields, "grp", split_axis=0, concat_axis=0, tiled=True, axis_index_groups=x_groups
    ).reshape(NX * rank, width + x_cols)
    fields, acts_t = lax.optimization_barrier((fields, acts_t))
    rows_in = to_owners(acts_t)
    first_all, second_all = fields[:, :width], fields[:, width:]
    second_wide = second_all.astype(F32)

    owner = jnp.arange(NX * rank, dtype=jnp.int32) // rank
    gram = jnp.where(
        owner[:, None] == owner[None, :], dot(first_all, first_all, ((1,), (1,))), 0.0
    )
    gram_second = dot(gram, second_wide, ((1,), (0,)), HIGH)
    first_weight = dot(first_all, weight_x, ((1,), (1,)))
    square_base = jnp.sum(jnp.square(weight_x.astype(F32)), axis=1)
    squares = square_base[None, :] + jnp.sum(
        (second_wide * (2.0 * first_weight + gram_second)).reshape(NX, rank, x_cols), axis=1
    )
    first_merged = first_weight + gram_second
    rows_low = dot(first_t, rows_in, ((1,), (1,)))

    def lanes(values):
        return jnp.concatenate(
            [values[:, i : i + 128] for i in range(0, values.shape[1], 128)], axis=0
        )

    pieces = first_merged.astype(BF).reshape(NX, rank, quads, t_cols)
    pieces = pieces.transpose(0, 2, 1, 3).reshape(shards, rank, t_cols)
    pieces = jnp.concatenate([pieces[:, :, i : i + 128] for i in range(0, t_cols, 128)], axis=1)
    square_upper, square_lower = split_pair(squares)
    common = jnp.concatenate(
        [lanes(square_upper), lanes(square_lower), lanes(rows_low.astype(BF))], axis=0
    )
    sums = jnp.concatenate(
        [pieces, jnp.broadcast_to(common[None], (shards,) + common.shape)], axis=1
    )
    sums = lax.all_to_all(sums, "tp", split_axis=0, concat_axis=0, tiled=True)
    sums = jnp.sum(sums.astype(F32), axis=0)

    def unlanes(values, height):
        return jnp.concatenate(
            [values[i : i + height] for i in range(0, values.shape[0], height)], axis=1
        )

    n_piece = rank * t_cols // 128
    n_square = NX * x_cols // 128
    merged_piece = unlanes(sums[:n_piece], rank)
    square_sum = unlanes(
        sums[n_piece : n_piece + n_square] + sums[n_piece + n_square : n_piece + 2 * n_square], NX
    )
    rows_low = unlanes(sums[n_piece + 2 * n_square :], rank)

    square_own = lax.all_to_all(
        square_sum.reshape(NX, 1, x_cols),
        "grp",
        split_axis=0,
        concat_axis=0,
        tiled=True,
        axis_index_groups=x_groups,
    ).reshape(1, out_width)
    swap = []
    for i in range(NX):
        for j in range(nz):
            for a in range(NX):
                for q in range(quads):
                    swap.append(
                        ((i * nz + j) * shards + a * quads + q, (a * nz + j) * shards + i * quads + q)
                    )
    merged_own = lax.ppermute(merged_piece, ("grp", "tp"), swap)
    norm = jnp.sqrt(square_own + EPSILON)
    scale = magnitude / norm

    def along_x(values, step):
        pairs = [
            (((i + step) % NX) * nz + j, i * nz + j) for i in range(NX) for j in range(nz)
        ]
        return lax.ppermute(values, "grp", pairs)

    after = along_x(weight_x, 1)
    before = along_x(weight_x, -1)
    half = x_cols // 2
    across = jnp.concatenate([along_x(after[:half], 1), along_x(before[half:], -1)], axis=0)
    pieces = ((weight_x, 0), (after, 1), (before, 3), (across, 2))
    blocks = [(my_x + step) % NX for _, step in pieces]
    weights = [piece for piece, _ in pieces]

    p_chips = ny // NX
    wide = 2 * t_cols

    def chip(step, place):
        return place[0] * p_chips + step

    def ring(step, place):
        return (chip(step, place) - place[1] + ny) % ny

    grad_spec = pl.BlockSpec((1, packed, t_cols), lambda i, place: (ring(i, place), 0, 0))
    weight_spec = pl.BlockSpec((wide, width), lambda i, place: (i, 0))
    across_spec = pl.BlockSpec((1, wide), lambda i, place: (0, chip(i, place)))

    def whole(*shape):
        return pl.BlockSpec(shape, lambda i, place: (0,) * len(shape))

    def where(block):
        return jnp.stack([block, my_t // 2, my_t % 2]).astype(jnp.int32)

    total, low = jnp.zeros((packed, width), F32), jnp.zeros((packed, rank), F32)
    for piece, block in zip(weights, blocks):
        total, low = pl.pallas_call(
            main_kernel,
            grid_spec=pltpu.PrefetchScalarGridSpec(
                num_scalar_prefetch=1,
                grid=(p_chips,),
                in_specs=[
                    across_spec,
                    pl.BlockSpec((rank, wide), lambda i, place: (0, chip(i, place))),
                    weight_spec,
                    grad_spec,
                    grad_spec,
                    whole(packed, width),
                    whole(packed, rank),
                ],
                out_specs=[whole(packed, width), whole(packed, rank)],
            ),
            out_shape=[
                jax.ShapeDtypeStruct((packed, width), F32),
                jax.ShapeDtypeStruct((packed, rank), F32),
            ],
            name="hidden_weight",
        )(where(block), scale, second, piece, mine, other, total, low)

    inner = low.astype(BF)
    back = (total + dot(inner, first, ((1,), (1,)))).astype(BF)
    back = to_owners(back)
    row_grad = dot(place, back, ((0,), (0,))).astype(BF)

    align = jnp.zeros((1, out_width), F32)
    for piece, block in zip(weights, blocks):
        part = pl.pallas_call(
            align_kernel,
            grid_spec=pltpu.PrefetchScalarGridSpec(
                num_scalar_prefetch=1,
                grid=(p_chips,),
                in_specs=[whole(packed, width), weight_spec, grad_spec, grad_spec],
                out_specs=pl.BlockSpec((1, wide), lambda i, place: (0, i)),
            ),
            out_shape=jax.ShapeDtypeStruct((1, x_cols), F32),
            name="align_columns",
        )(where(block), rows_in, piece, mine, other)
        align = lax.dynamic_update_slice(align, part, (0, block * x_cols))
    second_t = lax.dynamic_slice(second, (0, my_t * t_cols), (rank, t_cols)).astype(F32)
    first_moment = dot(rows_low.astype(BF), rows_grad_t, ((1,), (0,)))
    align_low = jnp.sum(first_moment * second_t, axis=0)
    align_t = lax.dynamic_slice(align, (0, my_t * t_cols), (1, t_cols)) + align_low
    align = lax.dynamic_update_slice(align, align_t, (0, my_t * t_cols))
    align = align.reshape(-1, 128)
    flip = 1
    while flip < shards:
        align = align + lax.ppermute(align, "tp", [(i, i ^ flip) for i in range(shards)])
        flip *= 2
    align = align.reshape(1, out_width)
    grad_gain = align / norm
    shrink = magnitude * align / (norm * norm * norm)

    shrunk = (second.astype(F32) * shrink).astype(BF)
    small = dot(second, shrunk, ((1,), (1,)))
    grad_a = dot(inner, rows_in, ((0,), (0,))) - dot(small.astype(BF), first_t, ((0,), (0,)))
    for piece, block in zip(weights, blocks):
        part = lax.dynamic_slice(shrunk, (0, block * x_cols), (rank, x_cols))
        grad_a = grad_a - dot(part, piece, ((1,), (0,)))
    scale_t = lax.dynamic_slice(scale, (0, my_t * t_cols), (1, t_cols))
    shrink_t = lax.dynamic_slice(shrink, (0, my_t * t_cols), (1, t_cols))
    grad_b = first_moment * scale_t - merged_own * shrink_t
    return row_grad, grad_a.T[None], grad_b[None], grad_gain


def solution(mesh):
    in_specs = (
        P("grp", "tp"),
        P("grp", None),
        P("grp", None),
        P(),
        P("tp", "grp"),
        P("grp", "tp", None),
        P("grp", None, None),
        P("grp", None),
    )
    out_specs = (P("grp", "tp"), P("grp", "tp", None), P("grp", None, "tp"), P("grp", None))
    return jax.shard_map(
        on_device, mesh=mesh, in_specs=in_specs, out_specs=out_specs, check_vma=False
    )
```

```python
import jax
import jax.numpy as jnp
from jax import lax
from jax.experimental import pallas as pl
from jax.experimental.pallas import tpu as pltpu
from jax.sharding import PartitionSpec as P

CAP = 12
NX = 4
EPSILON = 1e-06
BF = jnp.bfloat16
F32 = jnp.float32


def dot(left, right, dims, precision=None):
    return lax.dot_general(
        left, right, (dims, ((), ())), precision=precision, preferred_element_type=F32
    )


def row_targets(count_row, owner_slot, rows):
    ends = jnp.cumsum(count_row)
    starts = ends - count_row
    ids = jnp.arange(rows, dtype=jnp.int32)[None, :]
    inside = ((ids >= starts[:, None]) & (ids < ends[:, None])).astype(jnp.int32)
    shift = owner_slot * CAP - starts
    return jnp.sum(inside * shift[:, None], axis=0) + ids[0]


def align_kernel(place, rows_in, rows_low, weight, second, mine, other, joined, align, moment):
    z_cols = mine.shape[2]
    near = place[1] * z_cols
    for start, part in ((near, mine), (z_cols - near, other)):
        cols = pl.ds(pl.multiple_of(start, z_cols), z_cols)
        joined[:, cols] = part[0]
        products = dot(rows_low[...], part[0], ((0,), (0,)))
        moment[:, cols] = products
        projected = dot(rows_in[...], weight[cols, :], ((1,), (1,)))
        sums = jnp.sum(part[0].astype(F32) * projected, axis=0, keepdims=True)
        sums += jnp.sum(products * second[:, cols], axis=0, keepdims=True)
        align[:, cols] = sums


def on_device(acts, grads, counts, owner_slot, base_weight, adapter_a, adapter_b, magnitude):
    groups, shards = lax.axis_size("grp"), lax.axis_size("tp")
    nz = groups // NX
    rows, width = acts.shape
    out_width = grads.shape[1]
    rank = adapter_a.shape[2]
    t_cols, g_cols = out_width // shards, out_width // groups
    packed = groups * CAP
    z_cols = out_width // nz
    z_groups = [[i * nz + j for j in range(nz)] for i in range(NX)]
    x_groups = [[i * nz + j for i in range(NX)] for j in range(nz)]
    my_t = lax.axis_index("tp")
    my_part, my_core = my_t // 2 % (nz // 2), my_t % 2

    def exchange(values, axis, members=None):
        return lax.all_to_all(
            values, axis, split_axis=0, concat_axis=0, tiled=True, axis_index_groups=members
        )

    def to_owners(values):
        values = exchange(values.reshape(groups, CAP, values.shape[1]), "grp")
        return values.reshape(packed, values.shape[2])

    def arriving(values):
        values = values.reshape(-1, NX, nz, g_cols).transpose(0, 2, 1, 3)
        return values.reshape(-1, out_width)

    def natural(values):
        values = values.reshape(-1, nz, NX, g_cols).transpose(0, 2, 1, 3)
        return values.reshape(-1, out_width)

    shard = base_weight.T
    near = exchange(jnp.broadcast_to(shard[None], (NX,) + shard.shape), "grp", x_groups)
    weight = lax.all_gather(
        near.reshape(NX * g_cols, width), "grp", axis=0, tiled=True, axis_index_groups=z_groups
    )

    target = row_targets(counts[0], owner_slot, rows)
    place = (jnp.arange(packed, dtype=jnp.int32)[:, None] == target[None, :]).astype(BF)
    strip = lax.dynamic_slice(
        grads.reshape(rows, NX, nz, g_cols), (0, 0, my_t % nz, 0), (rows, NX, 1, g_cols)
    ).reshape(rows, z_cols)
    both = dot(place, jnp.concatenate([acts, strip], axis=1), ((1,), (0,))).astype(BF)
    both, near = lax.optimization_barrier((both, near))
    both = to_owners(both)
    rows_in, rows_grad_t = both[:, :width], both[:, width:]

    def along_y(values, step):
        pairs = [((i + 2 * step) % shards, i) for i in range(shards)]
        return lax.ppermute(values, "tp", pairs)

    n_parts, half = nz // 2, packed // 2
    above, below = along_y(rows_grad_t, 1), along_y(rows_grad_t, -1)
    far = jnp.concatenate([along_y(above[:half], 1), along_y(below[half:], -1)], axis=0)
    mine = jnp.stack([rows_grad_t, above, far, below])
    other = lax.ppermute(mine, "tp", [(i, i ^ 1) for i in range(shards)])

    first, second = adapter_a[0], arriving(adapter_b[0])
    first_t = first.T
    second_wide = second.astype(F32)
    gain = arriving(magnitude)
    gram = dot(first, first, ((0,), (0,)))
    gram_second = dot(gram, second_wide, ((1,), (0,)), lax.Precision.HIGHEST)
    rows_low = dot(rows_in, first, ((1,), (0,))).astype(BF)

    def lanes(values):
        return jnp.concatenate(
            [values[:, i : i + 128] for i in range(0, values.shape[1], 128)], axis=0
        )

    def unlanes(values, height):
        return jnp.concatenate(
            [values[i : i + height] for i in range(0, values.shape[0], height)], axis=1
        )

    def summed(values):
        return jnp.sum(exchange(values, "tp").astype(F32), axis=0)

    def to_all(values):
        return jnp.broadcast_to(values[None], (shards,) + values.shape)

    first_weight = dot(first_t, weight, ((1,), (1,)))
    square_base = jnp.sum(jnp.square(weight.astype(F32)), axis=1)
    squares = square_base[None, :] + jnp.sum(
        second_wide * (2.0 * first_weight + gram_second), axis=0, keepdims=True
    )

    wide = 2 * z_cols

    def fixed(*shape):
        return pl.BlockSpec(shape, lambda k, place: (0,) * len(shape))

    def chip(k, place):
        return lax.rem(place[0] + k, n_parts)

    block = pl.BlockSpec((1, packed, z_cols), lambda k, place: (k, 0, 0))
    rows_grad, align, first_moment = pl.pallas_call(
        align_kernel,
        grid_spec=pltpu.PrefetchScalarGridSpec(
            num_scalar_prefetch=1,
            grid=(n_parts,),
            in_specs=[
                fixed(packed, width),
                fixed(packed, rank),
                pl.BlockSpec((wide, width), lambda k, place: (chip(k, place), 0)),
                pl.BlockSpec((rank, wide), lambda k, place: (0, chip(k, place))),
                block,
                block,
            ],
            out_specs=[
                pl.BlockSpec((packed, wide), lambda k, place: (0, chip(k, place))),
                pl.BlockSpec((1, wide), lambda k, place: (0, chip(k, place))),
                pl.BlockSpec((rank, wide), lambda k, place: (0, chip(k, place))),
            ],
        ),
        out_shape=[
            jax.ShapeDtypeStruct((packed, out_width), BF),
            jax.ShapeDtypeStruct((1, out_width), F32),
            jax.ShapeDtypeStruct((rank, out_width), F32),
        ],
        compiler_params=pltpu.CompilerParams(vmem_limit_bytes=32 * 2**20),
        cost_estimate=pl.CostEstimate(
            flops=2 * packed * out_width * width,
            bytes_accessed=2 * out_width * (2 * packed + width),
            transcendentals=0,
        ),
        name="align_columns",
    )(jnp.stack([my_part, my_core]).astype(jnp.int32), rows_in, rows_low, weight, second_wide, mine, other)

    products = natural(jnp.concatenate([first_moment, first_weight + gram_second], axis=0))
    products = products.astype(BF)
    pieces = jnp.stack(
        [lanes(products[:, i : i + t_cols]) for i in range(0, out_width, t_cols)], axis=0
    )
    terms = jnp.concatenate([squares.reshape(-1, 128), align.reshape(-1, 128)], axis=0)
    n_terms = terms.shape[0]
    terms = summed(jnp.concatenate([to_all(terms.astype(BF)), pieces], axis=1))
    products = unlanes(terms[n_terms:], 2 * rank)
    moment_t, merged_t = products[:rank], products[rank:]
    terms = terms[:n_terms].reshape(2, out_width)
    norm = jnp.sqrt(terms[:1] + EPSILON)
    align = terms[1:]
    scale = gain / norm
    grad_gain = natural(align / norm)
    shrink = gain * align / (norm * norm * norm)

    hidden = (rows_grad.astype(F32) * scale).astype(BF)
    inner = dot(hidden, second, ((1,), (1,))).astype(BF)
    back = dot(hidden, weight, ((1,), (0,))) + dot(inner, first, ((1,), (1,)))
    row_grad = dot(place, to_owners(back.astype(BF)), ((0,), (0,))).astype(BF)

    shrunk = (second_wide * shrink).astype(BF)
    small = dot(second, shrunk, ((1,), (1,)))
    grad_a = (
        dot(inner, rows_in, ((0,), (0,)))
        - dot(shrunk, weight, ((1,), (0,)))
        - dot(small.astype(BF), first_t, ((0,), (0,)))
    )
    scale_t = lax.dynamic_slice(natural(scale), (0, my_t * t_cols), (1, t_cols))
    shrink_t = lax.dynamic_slice(natural(shrink), (0, my_t * t_cols), (1, t_cols))
    grad_b = moment_t * scale_t - merged_t * shrink_t
    return row_grad, grad_a.T[None], grad_b[None], grad_gain


def solution(mesh):
    in_specs = (
        P("grp", "tp"),
        P("grp", None),
        P("grp", None),
        P(),
        P("tp", "grp"),
        P("grp", "tp", None),
        P("grp", None, None),
        P("grp", None),
    )
    out_specs = (P("grp", "tp"), P("grp", "tp", None), P("grp", None, "tp"), P("grp", None))
    return jax.shard_map(
        on_device, mesh=mesh, in_specs=in_specs, out_specs=out_specs, check_vma=False
    )
```

```python
import jax
import jax.numpy as jnp
from jax import lax
from jax.experimental import pallas as pl
from jax.experimental.pallas import tpu as pltpu
from jax.sharding import PartitionSpec as P

CAP = 12
NX = 4
EPSILON = 1e-06
BF = jnp.bfloat16
F32 = jnp.float32


def dot(left, right, dims, precision=None):
    return lax.dot_general(
        left, right, (dims, ((), ())), precision=precision, preferred_element_type=F32
    )


def row_targets(count_row, owner_slot, rows):
    ends = jnp.cumsum(count_row)
    starts = ends - count_row
    ids = jnp.arange(rows, dtype=jnp.int32)[None, :]
    inside = ((ids >= starts[:, None]) & (ids < ends[:, None])).astype(jnp.int32)
    shift = owner_slot * CAP - starts
    return jnp.sum(inside * shift[:, None], axis=0) + ids[0]


def align_kernel(place, rows_in, rows_low, weight, second, mine, other, joined, align):
    z_cols = mine.shape[2]
    near = place[1] * z_cols
    for start, part in ((near, mine), (z_cols - near, other)):
        cols = pl.ds(pl.multiple_of(start, z_cols), z_cols)
        joined[:, cols] = part[0]
        projected = dot(rows_in[...], weight[cols, :], ((1,), (1,)))
        projected += jnp.dot(rows_low[...], second[:, cols], preferred_element_type=F32)
        align[:, cols] = jnp.sum(part[0].astype(F32) * projected, axis=0, keepdims=True)


def on_device(acts, grads, counts, owner_slot, base_weight, adapter_a, adapter_b, magnitude):
    groups, shards = lax.axis_size("grp"), lax.axis_size("tp")
    nz = groups // NX
    rows, width = acts.shape
    out_width = grads.shape[1]
    rank = adapter_a.shape[2]
    t_cols, g_cols = out_width // shards, out_width // groups
    packed = groups * CAP
    z_cols = out_width // nz
    z_groups = [[i * nz + j for j in range(nz)] for i in range(NX)]
    x_groups = [[i * nz + j for i in range(NX)] for j in range(nz)]
    my_t = lax.axis_index("tp")
    my_part, my_core = my_t // 2 % (nz // 2), my_t % 2

    def exchange(values, axis, members=None):
        return lax.all_to_all(
            values, axis, split_axis=0, concat_axis=0, tiled=True, axis_index_groups=members
        )

    def to_owners(values):
        values = exchange(values.reshape(groups, CAP, values.shape[1]), "grp")
        return values.reshape(packed, values.shape[2])

    def arriving(values):
        values = values.reshape(-1, NX, nz, g_cols).transpose(0, 2, 1, 3)
        return values.reshape(-1, out_width)

    def natural(values):
        values = values.reshape(-1, nz, NX, g_cols).transpose(0, 2, 1, 3)
        return values.reshape(-1, out_width)

    shard = base_weight.T
    near = exchange(jnp.broadcast_to(shard[None], (NX,) + shard.shape), "grp", x_groups)
    weight = lax.all_gather(
        near.reshape(NX * g_cols, width), "grp", axis=0, tiled=True, axis_index_groups=z_groups
    )

    target = row_targets(counts[0], owner_slot, rows)
    place = (jnp.arange(packed, dtype=jnp.int32)[:, None] == target[None, :]).astype(BF)
    strip = lax.dynamic_slice(
        grads.reshape(rows, NX, nz, g_cols), (0, 0, my_t % nz, 0), (rows, NX, 1, g_cols)
    ).reshape(rows, z_cols)
    both = dot(place, jnp.concatenate([acts, strip], axis=1), ((1,), (0,))).astype(BF)
    both, near = lax.optimization_barrier((both, near))
    both = to_owners(both)
    rows_in, rows_grad_t = both[:, :width], both[:, width:]

    def along_y(values, step):
        pairs = [((i + 2 * step) % shards, i) for i in range(shards)]
        return lax.ppermute(values, "tp", pairs)

    n_parts, half = nz // 2, packed // 2
    above, below = along_y(rows_grad_t, 1), along_y(rows_grad_t, -1)
    far = jnp.concatenate([along_y(rows_grad_t[:half], 2), along_y(rows_grad_t[half:], -2)], axis=0)
    mine = jnp.stack([rows_grad_t, above, far, below])
    other = lax.ppermute(mine, "tp", [(i, i ^ 1) for i in range(shards)])

    first, second = adapter_a[0], arriving(adapter_b[0])
    first_t = first.T
    second_wide = second.astype(F32)
    gain = magnitude.reshape(NX, nz, g_cols).transpose(1, 0, 2).reshape(-1, g_cols)
    gram = dot(first, first, ((0,), (0,)))
    gram_second = dot(gram, second_wide, ((1,), (0,)), lax.Precision.HIGHEST)
    rows_low = dot(rows_in, first, ((1,), (0,))).astype(BF)

    def lanes(values):
        return jnp.concatenate(
            [values[:, i : i + 128] for i in range(0, values.shape[1], 128)], axis=0
        )

    def unlanes(values, height):
        return jnp.concatenate(
            [values[i : i + height] for i in range(0, values.shape[0], height)], axis=1
        )

    def summed(values):
        return jnp.sum(exchange(values, "tp").astype(F32), axis=0)

    def to_all(values):
        return jnp.broadcast_to(values[None], (shards,) + values.shape)

    low_t = dot(first_t, rows_in, ((1,), (1,))).astype(BF)
    low_t = unlanes(summed(to_all(lanes(low_t))), rank).astype(BF)
    first_weight = dot(first_t, weight, ((1,), (1,)))
    square_base = jnp.sum(jnp.square(weight.astype(F32)), axis=1)
    squares = square_base[None, :] + jnp.sum(
        second_wide * (2.0 * first_weight + gram_second), axis=0, keepdims=True
    )

    wide = 2 * z_cols

    def fixed(*shape):
        return pl.BlockSpec(shape, lambda k, place: (0,) * len(shape))

    def chip(k, place):
        return lax.rem(place[0] + k, n_parts)

    block = pl.BlockSpec((1, packed, z_cols), lambda k, place: (k, 0, 0))
    rows_grad, align = pl.pallas_call(
        align_kernel,
        grid_spec=pltpu.PrefetchScalarGridSpec(
            num_scalar_prefetch=1,
            grid=(n_parts,),
            in_specs=[
                fixed(packed, width),
                fixed(packed, rank),
                pl.BlockSpec((wide, width), lambda k, place: (chip(k, place), 0)),
                pl.BlockSpec((rank, wide), lambda k, place: (0, chip(k, place))),
                block,
                block,
            ],
            out_specs=[
                pl.BlockSpec((packed, wide), lambda k, place: (0, chip(k, place))),
                pl.BlockSpec((1, wide), lambda k, place: (0, chip(k, place))),
            ],
        ),
        out_shape=[
            jax.ShapeDtypeStruct((packed, out_width), BF),
            jax.ShapeDtypeStruct((1, out_width), F32),
        ],
        compiler_params=pltpu.CompilerParams(vmem_limit_bytes=32 * 2**20),
        cost_estimate=pl.CostEstimate(
            flops=2 * packed * out_width * width,
            bytes_accessed=2 * out_width * (2 * packed + width),
            transcendentals=0,
        ),
        name="align_columns",
    )(jnp.stack([my_part, my_core]).astype(jnp.int32), rows_in, rows_low, weight, second, mine, other)

    products = natural(first_weight + gram_second)
    products = products.astype(BF)
    pieces = jnp.stack(
        [lanes(products[:, i : i + t_cols]) for i in range(0, out_width, t_cols)], axis=0
    )
    terms = jnp.concatenate([squares.reshape(-1, 128), align.reshape(-1, 128)], axis=0)
    n_terms = terms.shape[0]
    terms = summed(jnp.concatenate([to_all(terms.astype(BF)), pieces], axis=1))
    merged_t = unlanes(terms[n_terms:], rank)
    squares, align = terms[: n_terms // 2], terms[n_terms // 2 : n_terms]
    norm = jnp.sqrt(squares + EPSILON)
    scale = gain / norm
    shrink = gain * align / (norm * norm * norm)

    def in_order(values):
        values = values.reshape(nz, NX, g_cols).transpose(1, 0, 2)
        return values.reshape(groups, g_cols)

    grad_gain = in_order(align / norm).reshape(1, out_width)

    def along_tp(values):
        strips = t_cols // g_cols
        values = lax.dynamic_slice(in_order(values), (my_t * strips, 0), (strips, g_cols))
        return values.reshape(1, t_cols)

    hidden = (rows_grad.astype(F32) * scale.reshape(1, out_width)).astype(BF)
    inner = dot(hidden, second, ((1,), (1,))).astype(BF)
    back = dot(hidden, weight, ((1,), (0,))) + dot(inner, first, ((1,), (1,)))
    back, inner = lax.optimization_barrier((back.astype(BF), inner))
    row_grad = dot(place, to_owners(back), ((0,), (0,))).astype(BF)

    shrunk = (second_wide * shrink.reshape(1, out_width)).astype(BF)
    small = dot(second, shrunk, ((1,), (1,)))
    grad_a = (
        dot(inner, rows_in, ((0,), (0,)))
        - dot(shrunk, weight, ((1,), (0,)))
        - dot(small.astype(BF), first_t, ((0,), (0,)))
    )
    strips = []
    for i in range(t_cols // g_cols):
        block = my_t * (t_cols // g_cols) + i
        start = (block % nz * NX + block // nz) * g_cols
        strips.append(lax.dynamic_slice(rows_grad, (0, start), (packed, g_cols)))
    moment_t = dot(low_t, jnp.concatenate(strips, axis=1), ((1,), (0,)))
    grad_b = moment_t * along_tp(scale) - merged_t * along_tp(shrink)
    return row_grad, grad_a.T[None], grad_b[None], grad_gain


def solution(mesh):
    in_specs = (
        P("grp", "tp"),
        P("grp", None),
        P("grp", None),
        P(),
        P("tp", "grp"),
        P("grp", "tp", None),
        P("grp", None, None),
        P("grp", None),
    )
    out_specs = (P("grp", "tp"), P("grp", "tp", None), P("grp", None, "tp"), P("grp", None))
    return jax.shard_map(
        on_device, mesh=mesh, in_specs=in_specs, out_specs=out_specs, check_vma=False
    )
```

```python
import jax
import jax.numpy as jnp
from jax import lax
from jax.experimental import pallas as pl
from jax.experimental.pallas import tpu as pltpu
from jax.sharding import PartitionSpec as P

CAP = 12
NX = 4
EPSILON = 1e-06
BF = jnp.bfloat16
F32 = jnp.float32


def dot(left, right, dims, precision=None):
    return lax.dot_general(
        left, right, (dims, ((), ())), precision=precision, preferred_element_type=F32
    )


def row_targets(count_row, owner_slot, rows):
    ends = jnp.cumsum(count_row)
    starts = ends - count_row
    ids = jnp.arange(rows, dtype=jnp.int32)[None, :]
    inside = ((ids >= starts[:, None]) & (ids < ends[:, None])).astype(jnp.int32)
    shift = owner_slot * CAP - starts
    return jnp.sum(inside * shift[:, None], axis=0) + ids[0]


def columns_kernel(
    place, left, rows_low, weight, narrow, gram_second, mine, other, joined, terms, pieces
):
    packed, z_cols = mine.shape[1:]
    n_x, rank, g_cols = pieces.shape[0], rows_low.shape[1], pieces.shape[3]
    near = place[1] * z_cols
    ones = jnp.ones((8, weight.shape[1]), BF)
    for start, part in ((near, mine), (z_cols - near, other)):
        cols = pl.ds(pl.multiple_of(start, z_cols), z_cols)
        grads = part[0]
        joined[:, cols] = grads
        values = weight[cols, :]
        products = dot(left[...], values, ((1,), (1,)))
        first_weight = products[packed:]
        projected = products[:packed] + jnp.dot(
            rows_low[...], narrow[:, cols], preferred_element_type=F32
        )
        wide = values.astype(F32)
        wide = wide * wide
        upper = wide.astype(BF)
        lower = (wide - upper.astype(F32)).astype(BF)
        base = (dot(ones, upper, ((1,), (1,))) + dot(ones, lower, ((1,), (1,))))[:1]
        factor, extra = narrow[:, cols].astype(F32), gram_second[:, cols]
        terms[0:1, cols] = base + jnp.sum(
            factor * (2.0 * first_weight + extra), axis=0, keepdims=True
        )
        terms[1:2, cols] = jnp.sum(grads.astype(F32) * projected, axis=0, keepdims=True)
        merged = (first_weight + extra).astype(BF)
        strip = pl.multiple_of(start // z_cols * rank, rank)
        for i in range(n_x):
            strips = slice(i * g_cols, (i + 1) * g_cols)
            pieces[i, 0, pl.ds(strip, rank), :] = merged[:, strips]


def on_device(acts, grads, counts, owner_slot, base_weight, adapter_a, adapter_b, magnitude):
    groups, shards = lax.axis_size("grp"), lax.axis_size("tp")
    nz = groups // NX
    rows, width = acts.shape
    out_width = grads.shape[1]
    rank = adapter_a.shape[2]
    t_cols, g_cols = out_width // shards, out_width // groups
    packed = groups * CAP
    z_cols = out_width // nz
    z_groups = [[i * nz + j for j in range(nz)] for i in range(NX)]
    x_groups = [[i * nz + j for i in range(NX)] for j in range(nz)]
    my_t = lax.axis_index("tp")
    my_part, my_core = my_t // 2 % (nz // 2), my_t % 2

    def exchange(values, axis, members=None):
        return lax.all_to_all(
            values, axis, split_axis=0, concat_axis=0, tiled=True, axis_index_groups=members
        )

    def to_owners(values):
        values = exchange(values.reshape(groups, CAP, values.shape[1]), "grp")
        return values.reshape(packed, values.shape[2])

    def arriving(values):
        values = values.reshape(-1, NX, nz, g_cols).transpose(0, 2, 1, 3)
        return values.reshape(-1, out_width)

    def natural(values):
        values = values.reshape(-1, nz, NX, g_cols).transpose(0, 2, 1, 3)
        return values.reshape(-1, out_width)

    shard = base_weight.T
    near = exchange(jnp.broadcast_to(shard[None], (NX,) + shard.shape), "grp", x_groups)
    weight = lax.all_gather(
        near.reshape(NX * g_cols, width), "grp", axis=0, tiled=True, axis_index_groups=z_groups
    )

    target = row_targets(counts[0], owner_slot, rows)
    place = (jnp.arange(packed, dtype=jnp.int32)[:, None] == target[None, :]).astype(BF)
    strip = lax.dynamic_slice(
        grads.reshape(rows, NX, nz, g_cols), (0, 0, my_t % nz, 0), (rows, NX, 1, g_cols)
    ).reshape(rows, z_cols)
    both = dot(place, jnp.concatenate([acts, strip], axis=1), ((1,), (0,))).astype(BF)
    both, near = lax.optimization_barrier((both, near))
    both = to_owners(both)
    rows_in, rows_grad_t = both[:, :width], both[:, width:]

    def along_y(values, step):
        pairs = [((i + 2 * step) % shards, i) for i in range(shards)]
        return lax.ppermute(values, "tp", pairs)

    n_parts, half = nz // 2, packed // 2
    above, below = along_y(rows_grad_t, 1), along_y(rows_grad_t, -1)
    far = jnp.concatenate([along_y(rows_grad_t[:half], 2), along_y(rows_grad_t[half:], -2)], axis=0)
    mine = jnp.stack([rows_grad_t, above, far, below])
    first, second = adapter_a[0], arriving(adapter_b[0])
    first_t = first.T
    second_wide = second.astype(F32)
    gain = magnitude.reshape(NX, nz, g_cols).transpose(1, 0, 2).reshape(-1, g_cols)
    gram = dot(first, first, ((0,), (0,)))
    gram_second = dot(gram, second_wide, ((1,), (0,)), lax.Precision.HIGHEST)
    rows_low = dot(rows_in, first, ((1,), (0,))).astype(BF)

    left = jnp.concatenate([rows_in, first_t], axis=0)
    mine, left, rows_low, gram_second = lax.optimization_barrier(
        (mine, left, rows_low, gram_second)
    )
    other = lax.ppermute(mine, "tp", [(i, i ^ 1) for i in range(shards)])

    def lanes(values):
        return jnp.concatenate(
            [values[:, i : i + 128] for i in range(0, values.shape[1], 128)], axis=0
        )

    def unlanes(values, height):
        return jnp.concatenate(
            [values[i : i + height] for i in range(0, values.shape[0], height)], axis=1
        )

    def summed(values):
        return jnp.sum(exchange(values, "tp").astype(F32), axis=0)

    def to_all(values):
        return jnp.broadcast_to(values[None], (shards,) + values.shape)

    low_t = dot(first_t, rows_in, ((1,), (1,))).astype(BF)
    low_t = unlanes(summed(to_all(lanes(low_t))), rank).astype(BF)
    wide = 2 * z_cols

    def chip(k, place):
        return lax.rem(place[0] + k, n_parts)

    def fixed(*shape):
        return pl.BlockSpec(shape, lambda k, place: (0,) * len(shape))

    def across(height):
        return pl.BlockSpec((height, wide), lambda k, place: (0, chip(k, place)))

    block = pl.BlockSpec((1, packed, z_cols), lambda k, place: (k, 0, 0))
    rows_grad, terms, pieces = pl.pallas_call(
        columns_kernel,
        grid_spec=pltpu.PrefetchScalarGridSpec(
            num_scalar_prefetch=1,
            grid=(n_parts,),
            in_specs=[
                fixed(packed + rank, width),
                fixed(packed, rank),
                pl.BlockSpec((wide, width), lambda k, place: (chip(k, place), 0)),
                across(rank),
                across(rank),
                block,
                block,
            ],
            out_specs=[
                across(packed),
                across(2),
                pl.BlockSpec(
                    (NX, 1, 2 * rank, g_cols), lambda k, place: (0, chip(k, place), 0, 0)
                ),
            ],
        ),
        out_shape=[
            jax.ShapeDtypeStruct((packed, out_width), BF),
            jax.ShapeDtypeStruct((2, out_width), F32),
            jax.ShapeDtypeStruct((NX, n_parts, 2 * rank, g_cols), BF),
        ],
        compiler_params=pltpu.CompilerParams(vmem_limit_bytes=40 * 2**20),
        cost_estimate=pl.CostEstimate(
            flops=2 * packed * out_width * width,
            bytes_accessed=2 * out_width * (2 * packed + width),
            transcendentals=0,
        ),
        name="columns_sums",
    )(
        jnp.stack([my_part, my_core]).astype(jnp.int32),
        left,
        rows_low,
        weight,
        second,
        gram_second,
        mine,
        other,
    )

    terms = terms.astype(BF).reshape(-1, g_cols)
    n_terms = terms.shape[0]
    pieces = pieces.reshape(shards, 2 * rank, g_cols)
    terms = summed(jnp.concatenate([to_all(terms), pieces], axis=1))
    squares, align = terms[: n_terms // 2], terms[n_terms // 2 : n_terms]
    merged_t = unlanes(terms[n_terms:], rank)
    norm = jnp.sqrt(squares + EPSILON)
    scale = gain / norm
    shrink = gain * align / (norm * norm * norm)

    def in_order(values):
        values = values.reshape(nz, NX, g_cols).transpose(1, 0, 2)
        return values.reshape(groups, g_cols)

    grad_gain = in_order(align / norm).reshape(1, out_width)

    def along_tp(values):
        strips = t_cols // g_cols
        values = lax.dynamic_slice(in_order(values), (my_t * strips, 0), (strips, g_cols))
        return values.reshape(1, t_cols)

    hidden = (rows_grad.astype(F32) * scale.reshape(1, out_width)).astype(BF)
    inner = dot(hidden, second, ((1,), (1,))).astype(BF)
    back = dot(hidden, weight, ((1,), (0,))) + dot(inner, first, ((1,), (1,)))
    back, inner = lax.optimization_barrier((back.astype(BF), inner))
    row_grad = dot(place, to_owners(back), ((0,), (0,))).astype(BF)

    shrunk = (second_wide * shrink.reshape(1, out_width)).astype(BF)
    small = dot(second, shrunk, ((1,), (1,)))
    grad_a = (
        dot(inner, rows_in, ((0,), (0,)))
        - dot(shrunk, weight, ((1,), (0,)))
        - dot(small.astype(BF), first_t, ((0,), (0,)))
    )
    strips = []
    for i in range(t_cols // g_cols):
        block = my_t * (t_cols // g_cols) + i
        start = (block % nz * NX + block // nz) * g_cols
        strips.append(lax.dynamic_slice(rows_grad, (0, start), (packed, g_cols)))
    moment_t = dot(low_t, jnp.concatenate(strips, axis=1), ((1,), (0,)))
    grad_b = moment_t * along_tp(scale) - merged_t * along_tp(shrink)
    return row_grad, grad_a.T[None], grad_b[None], grad_gain


def solution(mesh):
    in_specs = (
        P("grp", "tp"),
        P("grp", None),
        P("grp", None),
        P(),
        P("tp", "grp"),
        P("grp", "tp", None),
        P("grp", None, None),
        P("grp", None),
    )
    out_specs = (P("grp", "tp"), P("grp", "tp", None), P("grp", None, "tp"), P("grp", None))
    return jax.shard_map(
        on_device, mesh=mesh, in_specs=in_specs, out_specs=out_specs, check_vma=False
    )
```
